32 devices in a mesh: dp: 4 (over y, core), seq: 2 (over x), tensor: 4 (over z).
Axes of the slice: x: 2, y: 2, z: 4, core: 2. Of those that a mesh axis runs over, the one named last changes fastest.
Arguments:
- queries: bfloat16 [16384, 8192], P(('dp', 'seq'), 'tensor'), parts along dimension 0, may hold values from -110 to 110
- keys_values: bfloat16 [16384, 2, 1024], P(('dp', 'seq'), None, 'tensor'), parts along dimension 0, may hold values from -4.5 to 4.5
- out_weight: bfloat16 [8192, 8192], P('tensor', 'seq'), may hold values from -0.1875 to 0.1875
- residual: bfloat16 [16384, 8192], P(('dp', 'tensor'), 'seq'), parts along dimension 0, may hold values from -3 to 3
- segments: int32 [16384], P('dp'), parts along dimension 0, may hold values from 0 to 3, never falling along the last dimension, each value on 1 to 2048 neighbouring positions
Outputs:
- layer_out: bfloat16 [16384, 8192], P(('dp', 'tensor'), 'seq'), parts along dimension 0
The draws below stay inside these ranges and needn't reach their ends.
There are 4 independent parts, one for each index of `dp`. The reference program is written for one: setup_inputs(seed, part) draws one part's arguments, and reference() takes and returns one part's arrays. A program takes and returns all parts, laid end to end along the dimension named above; an argument that names none is the same for every part. Nothing has to cross between parts.
Inputs may be any that keep to these rules, and one draw needn't show every extreme that they name: `segments`: segment numbers never fall along the tokens.
All inputs are finite; a program needn't handle non-finite values.
Results may differ from the reference program's by a relative error of at most 0.0085.
Values may be sent and summed in bfloat16 or wider, within the bound.
A program may use at most 384 MiB of HBM per device.

```python
import math
import jax
import jax.numpy as jnp
import numpy as np
from jax import lax

D = 8192
H = 64
KVH = 8
HD = 128
L = 4096
SEQS = 1
TOKENS = 4096


def shared_keys(key):
    drawn = jax.random.normal(jax.random.fold_in(key, 11), (TOKENS, 2, KVH * HD), jnp.float32)
    return jnp.clip(drawn, -4.5, 4.5)


def draw_keys_values(key, part):
    drawn = shared_keys(key)
    return drawn.astype(jnp.bfloat16)


def draw_queries(key, part):
    drawn = jax.random.normal(jax.random.fold_in(key, 12), (TOKENS, H * HD), jnp.float32)
    return jnp.clip(1.5 * drawn, -9.0, 9.0).astype(jnp.bfloat16)


def steps_of(rng, dims, cuts, low, largest):
    loudness = 1.0
    for axis_at, shards_of in cuts:
        draws = jax.random.uniform(jax.random.fold_in(jax.random.fold_in(rng, 6), axis_at), (shards_of,), jnp.float32, low / len(cuts), largest / len(cuts))
        loudness = loudness * jnp.repeat(jnp.exp(draws), dims[axis_at] // shards_of).reshape((-1,) + (1,) * (len(dims) - 1 - axis_at))
    return loudness


def profile(number_of, total, limit, skew):
    loads = [(1 << 20) // math.isqrt(grade ** skew) + 1 for grade in range(2, number_of + 1)]
    rest, counts = total - limit - (number_of - 1), [1] * (number_of - 1)
    while rest > 0:
        candidates = [i for i in range(number_of - 1) if counts[i] < limit]
        whole, left = sum([loads[i] for i in candidates]), rest
        for i in candidates:
            addition = min(limit - counts[i], max(1, left * loads[i] // whole), rest)
            counts[i] = counts[i] + addition
            rest = rest - addition
    return np.array([limit] + counts)


def uneven(key, amount, total, reach, slope):
    if amount == 2:
        one = jax.random.randint(key, (), max(1, total - reach), min(reach, total - 1) + 1)
        return jnp.stack([one, total - one])
    sizes = jnp.asarray(profile(amount, total, reach, slope), jnp.int32)
    pairs = (amount - 1) // 2
    donor, taker = sizes[1:1 + 2 * pairs:2], sizes[2:2 + 2 * pairs:2]
    margin = jnp.minimum(donor - 1, reach - taker)
    passed = jax.random.randint(jax.random.fold_in(key, 1), (pairs,), 0, 1 << 20) % (margin + 1)
    sizes = sizes.at[1:1 + 2 * pairs:2].set(donor - passed).at[2:2 + 2 * pairs:2].set(taker + passed)
    return sizes[jax.random.permutation(jax.random.fold_in(key, 2), amount)]


def bell_draw(key, extent, deviation, limit, shards=(), kind=jnp.bfloat16):
    result = deviation * jax.random.normal(key, extent, jnp.float32)
    if shards:
        result = result * steps_of(key, extent, shards, -0.22, 0.18)
    return jnp.clip(result, -limit, limit).astype(kind)


def setup_inputs(seed: int = 0, part: int = 0) -> dict:
    key_of = jax.random.split(jax.random.key(seed), 6)
    part_splits = jax.random.split(jax.random.fold_in(key_of[5], part), 6)
    queries = draw_queries(jax.random.fold_in(jax.random.fold_in(key_of[5], part), 71), part)
    keys_values = draw_keys_values(jax.random.fold_in(jax.random.fold_in(key_of[5], part), 71), part)
    out_weight = bell_draw(key_of[2], (H * HD, D), (H * HD // 8) ** -0.5, 0.1875, ((0, 4), (1, 2)))
    residual = bell_draw(part_splits[3], (TOKENS, D), 0.5, 3.0, ((0, 4), (1, 2)))
    segments = jnp.searchsorted(jnp.cumsum(uneven(part_splits[4], SEQS * 4, TOKENS, L // 2, 2)), jnp.arange(TOKENS), side="right").astype(jnp.int32)
    return dict(queries=queries, keys_values=keys_values, out_weight=out_weight, residual=residual, segments=segments)


def one_head(head, queries, keys_values, segments):
    group_size = H // KVH
    kv_head = head // group_size
    query_head = lax.dynamic_slice_in_dim(queries, head * HD, HD, 1).astype(jnp.float32).reshape(SEQS, L, HD)
    key_head = lax.dynamic_slice_in_dim(keys_values[:, 0, :], kv_head * HD, HD, 1).astype(jnp.float32).reshape(SEQS, L, HD)
    value_head = lax.dynamic_slice_in_dim(keys_values[:, 1, :], kv_head * HD, HD, 1).astype(jnp.float32).reshape(SEQS, L, HD)
    raw_scores = jnp.einsum("sqd,skd->sqk", query_head, key_head) * (HD ** -0.5)
    positions = jnp.arange(L, dtype=jnp.int32)
    causal = positions[None, :] <= positions[:, None]
    doc_ids = segments.reshape(SEQS, L)
    allowed = causal[None, :, :] & (doc_ids[:, :, None] == doc_ids[:, None, :])
    masked = jnp.where(allowed, raw_scores, -1e30)
    highest = jnp.max(masked, axis=-1, keepdims=True)
    exponents = jnp.where(allowed, jnp.exp(masked - highest), 0.0)
    weights = (exponents / jnp.sum(exponents, axis=-1, keepdims=True)).astype(jnp.bfloat16)
    blended = jnp.einsum("sqk,skd->sqd", weights.astype(jnp.float32), value_head)
    return blended.astype(jnp.bfloat16).reshape(SEQS * L, HD)


def reference(queries, keys_values, out_weight, residual, segments):
    stacked = lax.map(lambda head: one_head(head, queries, keys_values, segments), jnp.arange(H, dtype=jnp.int32))
    heads_out = jnp.transpose(stacked, (1, 0, 2)).reshape(SEQS * L, H * HD)
    projected = jnp.dot(heads_out, out_weight, preferred_element_type=jnp.float32)
    return (residual.astype(jnp.float32) + projected).astype(jnp.bfloat16)
```

```python
import functools

import jax
import jax.numpy as jnp
from jax import lax
from jax.experimental import pallas as pl
from jax.experimental.pallas import tpu as pltpu
from jax.sharding import PartitionSpec as P

H = 64
KVH = 8
HD = 128
L = 4096
NEG = -1e30
LOG2E = 1.4426950408889634


def attend_kernel(block, heads, starts_ref, q_ref, k_ref, vt_ref, first_ref, o_ref, m_ref, l_ref, acc_ref):
    at = pl.program_id(1)
    row0 = at * block
    low = starts_ref[2 * at] // block
    mid_low = jnp.minimum((starts_ref[2 * at + 1] + block - 1) // block, at)
    mid_low = jnp.maximum(mid_low, low)
    m_ref[...] = jnp.full(m_ref.shape, NEG, jnp.float32)
    l_ref[...] = jnp.zeros(l_ref.shape, jnp.float32)
    acc_ref[...] = jnp.zeros(acc_ref.shape, jnp.float32)
    scale = HD ** (-0.5) * LOG2E

    def step(masked, kb, carry):
        key0 = pl.multiple_of(kb * block, block)
        keys = k_ref[pl.ds(key0, block), :]
        values_t = vt_ref[:, pl.ds(key0, block)]
        if masked:
            key_pos = key0 + lax.broadcasted_iota(jnp.int32, (block, block), 0)
            query_pos = row0 + lax.broadcasted_iota(jnp.int32, (block, block), 1)
            allowed = (key_pos <= query_pos) & (key_pos >= first_ref[0:1, :])
        for head in range(heads):
            s = lax.dot_general(
                keys,
                q_ref[:, head * HD : (head + 1) * HD],
                (((1,), (1,)), ((), ())),
                preferred_element_type=jnp.float32,
            )
            s = s * scale
            if masked:
                s = jnp.where(allowed, s, NEG)
            m_old = m_ref[head : head + 1, :]
            m_new = jnp.maximum(m_old, jnp.max(s, axis=0, keepdims=True))
            alpha = jnp.exp2(m_old - m_new)
            p = jnp.exp2(s - m_new)
            l_ref[head : head + 1, :] = alpha * l_ref[head : head + 1, :] + jnp.sum(p, axis=0, keepdims=True)
            m_ref[head : head + 1, :] = m_new
            acc_ref[head] = alpha * acc_ref[head] + jnp.dot(
                values_t, p.astype(jnp.bfloat16), preferred_element_type=jnp.float32
            )
        return carry

    lax.fori_loop(low, mid_low, functools.partial(step, True), 0)
    lax.fori_loop(mid_low, at, functools.partial(step, False), 0)
    step(True, at, 0)
    for head in range(heads):
        blended = acc_ref[head] / l_ref[head : head + 1, :]
        o_ref[:, head * HD : (head + 1) * HD] = blended.T.astype(o_ref.dtype)


def attend(starts, query, keys, values_t, first, head0, count, group_size):
    rows = query.shape[0]
    block = 512
    heads = min(2, count)
    blocks = rows // block
    grid_spec = pltpu.PrefetchScalarGridSpec(
        num_scalar_prefetch=1,
        grid=(count // heads, blocks),
        in_specs=[
            pl.BlockSpec((block, heads * HD), lambda h, b, s: (b, head0 // heads + h)),
            pl.BlockSpec((rows, HD), lambda h, b, s: (0, (head0 + h * heads) // group_size)),
            pl.BlockSpec((HD, rows), lambda h, b, s: ((head0 + h * heads) // group_size, 0)),
            pl.BlockSpec((8, block), lambda h, b, s: (0, b)),
        ],
        out_specs=pl.BlockSpec((block, heads * HD), lambda h, b, s: (b, h)),
        scratch_shapes=[
            pltpu.VMEM((8, block), jnp.float32),
            pltpu.VMEM((8, block), jnp.float32),
            pltpu.VMEM((heads, HD, block), jnp.float32),
        ],
    )
    return pl.pallas_call(
        functools.partial(attend_kernel, block, heads),
        grid_spec=grid_spec,
        out_shape=jax.ShapeDtypeStruct((rows, count * HD), jnp.bfloat16),
        compiler_params=pltpu.CompilerParams(vmem_limit_bytes=32 * 1024 * 1024),
        cost_estimate=pl.CostEstimate(
            flops=4 * count * rows * rows * HD,
            bytes_accessed=4 * count * rows * HD,
            transcendentals=count * rows * rows // 2,
        ),
    )(starts, query, keys, values_t, first)


def shift(array, axis, by):
    size = lax.axis_size(axis)
    return lax.ppermute(array, axis, [(i, (i + by) % size) for i in range(size)])


def gather_weight(out_weight):
    n_dp, n_ten = lax.axis_size("dp"), lax.axis_size("tensor")
    dp, ten = lax.axis_index("dp"), lax.axis_index("tensor")
    rows, columns = out_weight.shape
    part = rows // n_dp
    half = part // 2
    forward = lax.dynamic_slice(out_weight, (dp * part, 0), (half, columns))
    back = lax.dynamic_slice(out_weight, (dp * part + half, 0), (half, columns))
    full = jnp.zeros((rows * n_ten, columns), out_weight.dtype)
    full = lax.dynamic_update_slice(full, out_weight, (ten * rows, 0))
    for k in range(1, n_ten):
        forward = shift(forward, "tensor", 1)
        back = shift(back, "tensor", -1)
        for piece, source, at in ((forward, ten - k + n_ten, 0), (back, ten + k, half)):
            base = lax.rem(source, n_ten) * rows + at
            held = [(piece, dp)]
            bit = n_dp // 2
            while bit:
                pairs = [(i, i ^ bit) for i in range(n_dp)]
                held = held + [(lax.ppermute(p, "dp", pairs), who ^ bit) for p, who in held]
                bit //= 2
            for p, who in held:
                full = lax.dynamic_update_slice(full, p, (base + who * part, 0))
    return full


def exchange_columns(array, width, start_of):
    n_seq, me = lax.axis_size("seq"), lax.axis_index("seq")
    rows = array.shape[0]
    result = jnp.zeros((rows * n_seq, width), array.dtype)
    for j in range(n_seq):
        target = lax.rem(me + j, n_seq)
        piece = lax.dynamic_slice(array, (0, start_of(target)), (rows, width))
        if j:
            piece = shift(piece, "seq", j)
        result = lax.dynamic_update_slice(result, piece, (lax.rem(me - j + n_seq, n_seq) * rows, 0))
    return result


def on_device(queries, keys_values, out_weight, residual, segments):
    n_seq, n_ten = lax.axis_size("seq"), lax.axis_size("tensor")
    seq, ten = lax.axis_index("seq"), lax.axis_index("tensor")
    heads_ten = queries.shape[1] // HD
    heads_dev = heads_ten // n_seq
    group_size = H // KVH
    kv_dev = max(1, heads_dev // group_size)
    width = heads_dev * HD

    def kv_start(target):
        return target * heads_dev // group_size * HD

    query = exchange_columns(queries, width, lambda target: target * width)
    keys = exchange_columns(keys_values[:, 0, :], kv_dev * HD, kv_start)
    values_t = exchange_columns(keys_values[:, 1, :], kv_dev * HD, kv_start).T
    rows = query.shape[0]
    positions = jnp.arange(rows, dtype=jnp.int32)
    begins = (positions % L == 0) | (segments != jnp.roll(segments, 1))
    first = lax.cummax(jnp.where(begins, positions, 0))
    first_rows = first.reshape(rows // 512, 512)
    starts = jnp.stack([first_rows[:, 0], first_rows[:, -1]], axis=1).reshape(-1)
    first = jnp.broadcast_to(first[None, :], (8, rows))

    weight = gather_weight(out_weight)

    out_rows = rows // n_ten
    cuts = 2 if heads_dev >= 4 else 1
    count = heads_dev // cuts
    left = jnp.zeros((out_rows, H * HD), jnp.bfloat16)
    for cut in range(cuts):
        blended = attend(starts, query, keys, values_t, first, cut * count, count, group_size)
        for k in range(n_ten):
            target = lax.rem(ten + k, n_ten)
            piece = lax.dynamic_slice(blended, (target * out_rows, 0), (out_rows, count * HD))
            if k:
                piece = shift(piece, "tensor", k)
            base = lax.rem(ten - k + n_ten, n_ten) * heads_ten * HD + cut * count * HD
            for j in range(n_seq):
                held = shift(piece, "seq", j) if j else piece
                source = lax.rem(seq - j + n_seq, n_seq)
                left = lax.dynamic_update_slice(left, held, (0, base + source * width))
    projected = jnp.dot(left, weight, preferred_element_type=jnp.float32)
    return (residual.astype(jnp.float32) + projected).astype(jnp.bfloat16)


def solution(mesh):
    placed = (
        P(("dp", "seq"), "tensor"),
        P(("dp", "seq"), None, "tensor"),
        P("tensor", "seq"),
        P(("dp", "tensor"), "seq"),
        P("dp"),
    )
    return jax.shard_map(
        on_device, mesh=mesh, in_specs=placed, out_specs=P(("dp", "tensor"), "seq"), check_vma=False
    )
```

```python
import functools

import jax
import jax.numpy as jnp
from jax import lax
from jax.experimental import pallas as pl
from jax.experimental.pallas import tpu as pltpu
from jax.sharding import PartitionSpec as P

H = 64
KVH = 8
HD = 128
L = 4096
NEG = -1e30
LOG2E = 1.4426950408889634


def attend_kernel(block, heads, starts_ref, q_ref, k_ref, vt_ref, first_ref, o_ref, m_ref, l_ref, acc_ref):
    at = pl.program_id(1)
    row0 = at * block
    low = starts_ref[2 * at] // block
    mid_low = jnp.minimum((starts_ref[2 * at + 1] + block - 1) // block, at)
    mid_low = jnp.maximum(mid_low, low)
    m_ref[...] = jnp.full(m_ref.shape, NEG, jnp.float32)
    l_ref[...] = jnp.zeros(l_ref.shape, jnp.float32)
    acc_ref[...] = jnp.zeros(acc_ref.shape, jnp.float32)
    scale = HD ** (-0.5) * LOG2E

    def step(masked, kb, carry):
        key0 = pl.multiple_of(kb * block, block)
        keys = k_ref[pl.ds(key0, block), :]
        values_t = vt_ref[:, pl.ds(key0, block)]
        if masked:
            key_pos = key0 + lax.broadcasted_iota(jnp.int32, (block, block), 0)
            query_pos = row0 + lax.broadcasted_iota(jnp.int32, (block, block), 1)
            allowed = (key_pos <= query_pos) & (key_pos >= first_ref[0:1, :])
        for head in range(heads):
            s = lax.dot_general(
                keys,
                q_ref[:, head * HD : (head + 1) * HD],
                (((1,), (1,)), ((), ())),
                preferred_element_type=jnp.float32,
            )
            s = s * scale
            if masked:
                s = jnp.where(allowed, s, NEG)
            m_old = m_ref[head : head + 1, :]
            m_new = jnp.maximum(m_old, jnp.max(s, axis=0, keepdims=True))
            alpha = jnp.exp2(m_old - m_new)
            p = jnp.exp2(s - m_new)
            l_ref[head : head + 1, :] = alpha * l_ref[head : head + 1, :] + jnp.sum(p, axis=0, keepdims=True)
            m_ref[head : head + 1, :] = m_new
            acc_ref[head] = alpha * acc_ref[head] + jnp.dot(
                values_t, p.astype(jnp.bfloat16), preferred_element_type=jnp.float32
            )
        return carry

    lax.fori_loop(low, mid_low, functools.partial(step, True), 0)
    lax.fori_loop(mid_low, at, functools.partial(step, False), 0)
    step(True, at, 0)
    for head in range(heads):
        blended = acc_ref[head] / l_ref[head : head + 1, :]
        o_ref[:, head * HD : (head + 1) * HD] = blended.T.astype(o_ref.dtype)


def attend(starts, query, keys, values_t, first, head0, count, group_size):
    rows = query.shape[0]
    block = 512
    heads = min(2, count)
    blocks = rows // block
    grid_spec = pltpu.PrefetchScalarGridSpec(
        num_scalar_prefetch=1,
        grid=(count // heads, blocks),
        in_specs=[
            pl.BlockSpec((block, heads * HD), lambda h, b, s: (b, h)),
            pl.BlockSpec((rows, HD), lambda h, b, s: (0, (head0 + h * heads) // group_size)),
            pl.BlockSpec((HD, rows), lambda h, b, s: ((head0 + h * heads) // group_size, 0)),
            pl.BlockSpec((8, block), lambda h, b, s: (0, b)),
        ],
        out_specs=pl.BlockSpec((block, heads * HD), lambda h, b, s: (b, h)),
        scratch_shapes=[
            pltpu.VMEM((8, block), jnp.float32),
            pltpu.VMEM((8, block), jnp.float32),
            pltpu.VMEM((heads, HD, block), jnp.float32),
        ],
    )
    return pl.pallas_call(
        functools.partial(attend_kernel, block, heads),
        grid_spec=grid_spec,
        out_shape=jax.ShapeDtypeStruct((rows, count * HD), jnp.bfloat16),
        compiler_params=pltpu.CompilerParams(vmem_limit_bytes=32 * 1024 * 1024),
        cost_estimate=pl.CostEstimate(
            flops=4 * count * rows * rows * HD,
            bytes_accessed=4 * count * rows * HD,
            transcendentals=count * rows * rows // 2,
        ),
    )(starts, query, keys, values_t, first)


def shift(array, axis, by):
    size = lax.axis_size(axis)
    return lax.ppermute(array, axis, [(i, (i + by) % size) for i in range(size)])


def share_of(mine):
    part = mine.shape[0] // lax.axis_size("dp")
    return lax.dynamic_slice(mine, (lax.axis_index("dp") * part, 0), (part, mine.shape[1]))


def spread_weight(mine, gathered):
    n_dp, n_ten = lax.axis_size("dp"), lax.axis_size("tensor")
    dp, ten = lax.axis_index("dp"), lax.axis_index("tensor")
    rows, columns = mine.shape
    part = rows // n_dp
    others = [lax.rem(ten + k, n_ten) for k in range(1, n_ten)]
    piece = jnp.concatenate(
        [lax.dynamic_slice(gathered, (other * part, 0), (part, columns)) for other in others]
    )
    held = [(piece, dp)]
    bit = n_dp // 2
    while bit:
        pairs = [(i, i ^ bit) for i in range(n_dp)]
        held = held + [(lax.ppermute(p, "dp", pairs), who ^ bit) for p, who in held]
        bit //= 2
    full = jnp.zeros((rows * n_ten, columns), mine.dtype)
    full = lax.dynamic_update_slice(full, mine, (ten * rows, 0))
    for p, who in held:
        for at, other in enumerate(others):
            full = lax.dynamic_update_slice(
                full, p[at * part : (at + 1) * part], (other * rows + who * part, 0)
            )
    return full


def exchange_columns(array, width, start_of):
    n_seq, me = lax.axis_size("seq"), lax.axis_index("seq")
    rows = array.shape[0]
    result = jnp.zeros((rows * n_seq, width), array.dtype)
    for j in range(n_seq):
        target = lax.rem(me + j, n_seq)
        piece = lax.dynamic_slice(array, (0, start_of(target)), (rows, width))
        if j:
            piece = shift(piece, "seq", j)
        result = lax.dynamic_update_slice(result, piece, (lax.rem(me - j + n_seq, n_seq) * rows, 0))
    return result


def on_device(queries, keys_values, out_weight, residual, segments):
    n_seq, n_ten = lax.axis_size("seq"), lax.axis_size("tensor")
    seq, ten = lax.axis_index("seq"), lax.axis_index("tensor")
    heads_ten = queries.shape[1] // HD
    heads_dev = heads_ten // n_seq
    group_size = H // KVH
    kv_dev = max(1, heads_dev // group_size)
    width = heads_dev * HD

    def kv_start(target):
        return target * heads_dev // group_size * HD

    keys = exchange_columns(keys_values[:, 0, :], kv_dev * HD, kv_start)
    values_t = exchange_columns(keys_values[:, 1, :], kv_dev * HD, kv_start).T
    rows = keys.shape[0]
    positions = jnp.arange(rows, dtype=jnp.int32)
    begins = (positions % L == 0) | (segments != jnp.roll(segments, 1))
    first = lax.cummax(jnp.where(begins, positions, 0))
    first_rows = first.reshape(rows // 512, 512)
    starts = jnp.stack([first_rows[:, 0], first_rows[:, -1]], axis=1).reshape(-1)
    first = jnp.broadcast_to(first[None, :], (8, rows))

    out_rows = rows // n_ten
    cuts = 2 if heads_dev >= 4 else 1
    count = heads_dev // cuts
    cut_width = count * HD
    by_cut = out_weight.reshape(n_seq, cuts, cut_width, out_weight.shape[1])
    mine = [by_cut[:, cut].reshape(n_seq * cut_width, out_weight.shape[1]) for cut in range(cuts)]
    gathered = lax.all_gather(share_of(mine[0]), "tensor", axis=0, tiled=True)
    total = residual.astype(jnp.float32)
    for cut in range(cuts):
        held_queries = lax.optimization_barrier((queries, keys))[0] if cut else queries
        query = exchange_columns(
            held_queries, cut_width, lambda target: target * width + cut * cut_width
        )
        blended = attend(starts, query, keys, values_t, first, cut * count, count, group_size)
        gathered = lax.optimization_barrier((gathered, blended))[0]
        ready = gathered
        if cut + 1 < cuts:
            share = lax.optimization_barrier((share_of(mine[cut + 1]), gathered))[0]
            gathered = lax.all_gather(share, "tensor", axis=0, tiled=True)
        weight = spread_weight(mine[cut], ready)
        left = jnp.zeros((out_rows, n_ten * n_seq * cut_width), jnp.bfloat16)
        for k in range(n_ten):
            target = lax.rem(ten + k, n_ten)
            piece = lax.dynamic_slice(blended, (target * out_rows, 0), (out_rows, cut_width))
            if k:
                piece = shift(piece, "tensor", k)
            base = lax.rem(ten - k + n_ten, n_ten) * n_seq * cut_width
            for j in range(n_seq):
                held = shift(piece, "seq", j) if j else piece
                source = lax.rem(seq - j + n_seq, n_seq)
                left = lax.dynamic_update_slice(left, held, (0, base + source * cut_width))
        total = total + jnp.dot(left, weight, preferred_element_type=jnp.float32)
    return total.astype(jnp.bfloat16)


def solution(mesh):
    placed = (
        P(("dp", "seq"), "tensor"),
        P(("dp", "seq"), None, "tensor"),
        P("tensor", "seq"),
        P(("dp", "tensor"), "seq"),
        P("dp"),
    )
    return jax.shard_map(
        on_device, mesh=mesh, in_specs=placed, out_specs=P(("dp", "tensor"), "seq"), check_vma=False
    )
```
